32 devices in a mesh: groups: 2 (over y), gy: 4 (over z), gx: 2 (over x), orb: 2 (over core).
Axes of the slice: x: 2, y: 2, z: 4, core: 2. Of those that a mesh axis runs over, the one named last changes fastest.
Arguments:
- checkpoint: float32 [4, 32, 40, 512], P('groups', 'gy', 'gx', 'orb'), parts along dimension 0, may hold values from -6 to 6
- cotangent: float32 [4, 32, 40, 512], P('groups', 'gy', 'gx', 'orb'), parts along dimension 0, may hold values from -6 to 6
- onsite: float32 [64, 40], P(('groups', 'gy'), 'gx'), parts along dimension 0, may hold values from -1.5 to 1.5
- bond_class: int32 [4, 32, 40], P('groups', 'gy', 'gx'), parts along dimension 0, may hold values from 0 to 15
- bond_table: float32 [16, 4], replicated, may hold values from -3 to 3
- occupied: int32 [1024], P(('groups', 'orb')), parts along dimension 0, may hold values 0 or 1
Outputs:
- adjoint_start: float32 [4, 32, 40, 512], P('groups', 'gy', 'gx', 'orb'), parts along dimension 0
- bond_gradient: float32 [16, 32, 40], P(('groups', 'orb'), 'gy', 'gx'), parts along dimension 0
The draws below stay inside these ranges and needn't reach their ends.
There are 2 independent parts, one for each index of `groups`. The reference program is written for one: setup_inputs(seed, part) draws one part's arguments, and reference() takes and returns one part's arrays. A program takes and returns all parts, laid end to end along the dimension named above; an argument that names none is the same for every part. Nothing has to cross between parts.
All inputs are finite; a program needn't handle non-finite values. No bound on the sum of `occupied` on one device may be relied on, other than what follows from the above.
Results may differ from the reference program's by a relative error of at most 0.00012.
Values sent between devices are 32-bit elements; how exact they have to be, the bound alone decides.
A program may use at most 64 MiB of HBM per device.

```python
import jax
import jax.numpy as jnp
from jax import lax

K = 512
NCLASS = 16
NX = 32
NY = 40


def draw_bond_table(key, part):
    key = jax.random.fold_in(key, 7)
    sign_key, size_key = jax.random.split(key)
    flips = jax.random.randint(sign_key, (NCLASS, 4), 0, 2).astype(jnp.float32)
    signs = 2.0 * flips - 1.0
    lowest = 2.4
    magnitude = jax.random.uniform(size_key, (NCLASS, 4), jnp.float32, lowest, 3.0)
    return (signs * magnitude).astype(jnp.float32)


def plant(values, stream_key, low, top_value):
    dims = values.shape
    place = [jax.random.randint(jax.random.fold_in(stream_key, axis), (), 0, dims[axis]) for axis in range(len(dims))]
    values = values.at[tuple(place)].set(low)
    longest = dims.index(max(dims))
    place[longest] = (place[longest] + 1) % dims[longest]
    return values.at[tuple(place)].set(top_value)


def block_levels(rng, extent, shards, low, high):
    def one(dim, shards_of):
        heights = jax.random.uniform(jax.random.fold_in(jax.random.fold_in(rng, 6), dim), (shards_of,), jnp.float32, low / len(shards), high / len(shards))
        return jnp.repeat(jnp.exp(heights), extent[dim] // shards_of).reshape((-1,) + (1,) * (len(extent) - dim - 1))

    level = one(*shards[0])
    for cut in shards[1:]:
        level = level * one(*cut)
    return level


def centred(own_key, shape, deviation, reach, cuts=(), held_as=jnp.bfloat16):
    drawn = deviation * jax.random.normal(own_key, shape, jnp.float32)
    if cuts:
        drawn = drawn * block_levels(own_key, shape, cuts, -0.22, 0.18)
    return jnp.clip(drawn, -reach, reach).astype(held_as)


def setup_inputs(seed: int = 0, part: int = 0) -> dict:
    keys = jax.random.split(jax.random.key(seed), 7)
    part_splits = jax.random.split(jax.random.fold_in(keys[6], part), 7)
    checkpoint = centred(part_splits[0], (2, NX, NY, K), 1.0, 6.0, ((1, 4), (2, 2), (3, 2)), jnp.float32)
    cotangent = centred(part_splits[1], (2, NX, NY, K), 1.0, 6.0, ((1, 4), (2, 2), (3, 2)), jnp.float32)
    onsite = jnp.clip(jax.random.uniform(part_splits[2], (NX, NY), jnp.float32, -1.5, 1.5) * block_levels(part_splits[2], (NX, NY), ((0, 4), (1, 2)), -0.4, 0.0), -1.5, 1.5)
    bond_class = plant(jax.random.randint(part_splits[3], (2, NX, NY), 0, NCLASS), jax.random.fold_in(part_splits[3], 1), 0, NCLASS - 1).astype(jnp.int32)
    bond_table = draw_bond_table(jax.random.fold_in(keys[6], 71), part)
    occupied = plant((jax.random.randint(part_splits[5], (K,), 0, 2) < 1).astype(jnp.int32), jax.random.fold_in(part_splits[5], 1), 0, 1)
    return {"checkpoint": checkpoint, "cotangent": cotangent, "onsite": onsite, "bond_class": bond_class, "bond_table": bond_table, "occupied": occupied}


time_step = 0.1
half_step = 0.05

def combine(center, right, left, down, up, mu, bh, bhl, bv, bvu):
    out0 = mu * center[1] + bh[0] * right[0] + bh[1] * right[1] + bv[0] * down[0] + bv[1] * down[1] - bhl[0] * left[0] - bhl[2] * left[1] - bvu[0] * up[0] - bvu[2] * up[1]
    out1 = -mu * center[0] + bh[2] * right[0] + bh[3] * right[1] + bv[2] * down[0] + bv[3] * down[1] - bhl[1] * left[0] - bhl[3] * left[1] - bvu[1] * up[0] - bvu[3] * up[1]
    return jnp.stack([out0, out1])

def generator(field, coefs):
    mu, bh, bhl, bv, bvu = coefs
    right = jnp.roll(field, -1, axis=2)
    left = jnp.roll(field, 1, axis=2)
    down = jnp.roll(field, -1, axis=1)
    upper = jnp.roll(field, 1, axis=1)
    return combine(field, right, left, down, upper, mu, bh, bhl, bv, bvu)

def pair_grad(lam, val):
    hp = lax.Precision.HIGHEST
    lam_r = jnp.roll(lam, -1, axis=2)
    val_r = jnp.roll(val, -1, axis=2)
    lam_d = jnp.roll(lam, -1, axis=1)
    val_d = jnp.roll(val, -1, axis=1)
    horiz = jnp.einsum('aijk,bijk->abij', lam, val_r, precision=hp) - jnp.einsum('aijk,bijk->abij', val, lam_r, precision=hp)
    vert = jnp.einsum('aijk,bijk->abij', lam, val_d, precision=hp) - jnp.einsum('aijk,bijk->abij', val, lam_d, precision=hp)
    return jnp.concatenate([horiz.reshape(4, NX, NY), vert.reshape(4, NX, NY)], axis=0)

def reference(checkpoint, cotangent, onsite, bond_class, bond_table, occupied):
    looked = jnp.transpose(bond_table[bond_class], (0, 3, 1, 2))
    bh = looked[0][:, :, :, None]
    bv = looked[1][:, :, :, None]
    bhl = jnp.roll(bh, 1, axis=2)
    bvu = jnp.roll(bv, 1, axis=1)
    mu = onsite[:, :, None]
    coefs = (mu, bh, bhl, bv, bvu)
    width = 128 if K % 128 == 0 else K
    nblock = K // width
    signs = (2 * occupied - 1).astype(jnp.float32).reshape(nblock, width)
    starts = jnp.transpose(checkpoint.reshape(2, NX, NY, nblock, width), (3, 0, 1, 2, 4))
    cots = jnp.transpose(cotangent.reshape(2, NX, NY, nblock, width), (3, 0, 1, 2, 4))

    def one_block(items):
        x0, cot, sign = items
        y0 = x0 + half_step * generator(x0, coefs)
        x1 = x0 + time_step * generator(y0, coefs)
        y1 = x1 + half_step * generator(x1, coefs)
        l2 = cot * sign
        ly1 = -time_step * generator(l2, coefs)
        l1 = l2 + ly1 - half_step * generator(ly1, coefs)
        ly0 = -time_step * generator(l1, coefs)
        l0 = l1 + ly0 - half_step * generator(ly0, coefs)
        late = time_step * pair_grad(l2, y1) + half_step * pair_grad(ly1, x1)
        early = time_step * pair_grad(l1, y0) + half_step * pair_grad(ly0, x0)
        return (l0, late + early)
    ends, grads = lax.map(one_block, (starts, cots, signs))
    adjoint_start = jnp.transpose(ends, (1, 2, 3, 0, 4)).reshape(2, NX, NY, K)
    return (adjoint_start, lax.optimization_barrier(jnp.sum(grads, axis=0)))
```

```python
import functools

import jax
import jax.numpy as jnp
from jax import lax
from jax.experimental import pallas as pl
from jax.experimental.pallas import tpu as pltpu
from jax.sharding import PartitionSpec as P

half_step = 0.05
DEPTH = 4
MESH = pl.DeviceIdType.MESH
ROW_SIDES = ((-1, 0), (1, 0))
COL_SIDES = ((0, -1), (0, 1))
CORNERS = ((-1, -1), (-1, 1), (1, -1), (1, 1))
SIDES = ROW_SIDES + COL_SIDES + CORNERS
X0, Y0, X1, Y1, L2, LY1, L1, LY0 = range(8)


def kernel(
    sizes, x_hbm, c_hbm, onsite_ref, class_ref, table_ref, occ_ref,
    out_ref, grad_ref,
    own, fields, cf, tab, acc, part, part_in,
    send_rows, recv_rows, send_cols, recv_cols, send_corn, recv_corn,
    meta, meta_in, meta_pad,
    copy_sem, send_sem, recv_sem,
):
    gy_n, gx_n, orb_n, rows, cols, width = sizes
    halves = width // 128
    gy, gx, orb = lax.axis_index("gy"), lax.axis_index("gx"), lax.axis_index("orb")
    d = DEPTH
    left0 = 8 - d
    tail = cols - 16

    def at(si, sj):
        return {
            "gy": lax.rem(gy + si + gy_n, gy_n),
            "gx": lax.rem(gx + sj + gx_n, gx_n),
        }

    other = {"orb": lax.rem(orb + 1, orb_n)}

    loads = [
        pltpu.make_async_copy(src, own.at[f], copy_sem.at[f])
        for f, src in enumerate((x_hbm, c_hbm))
    ]
    for load in loads:
        load.start()

    barrier = pltpu.get_barrier_semaphore()
    for si, sj in SIDES:
        pl.semaphore_signal(barrier, inc=1, device_id=at(si, sj), device_id_type=MESH)
    pl.semaphore_signal(barrier, inc=1, device_id=other, device_id_type=MESH)

    meta[0:rows, 0:cols] = class_ref[0].astype(jnp.float32)
    meta[rows : 2 * rows, 0:cols] = class_ref[1].astype(jnp.float32)
    meta[2 * rows : 3 * rows, 0:cols] = half_step * onsite_ref[...]
    sign = (2 * occ_ref[...] - 1).astype(jnp.float32)

    zero = jnp.zeros((16, 128), jnp.float32)
    for e in range(4):
        t = jnp.broadcast_to(half_step * table_ref[:, e : e + 1], (16, 128))
        high = t.astype(jnp.bfloat16)
        rest = t - high.astype(jnp.float32)
        mid = rest.astype(jnp.bfloat16)
        low = (rest - mid.astype(jnp.float32)).astype(jnp.bfloat16)
        lanes = slice(e * 128, e * 128 + 128)
        tab[0:16, lanes] = high
        tab[16:32, lanes] = mid
        tab[32:48, lanes] = low
        tab[48:64, lanes] = zero.astype(jnp.bfloat16)
    tab[0:48, 512:640] = jnp.zeros((48, 128), jnp.bfloat16)
    tab[48:64, 512:640] = jnp.ones((16, 128), jnp.bfloat16)

    def pack(f, scale):
        def rows_of(side, first):
            def body(q, carry):
                for c in range(2):
                    v = own[f, c, first + q] * scale
                    send_rows[f, side, q, 16 * c : 16 * c + 16, :] = v[0:16]
                    send_rows[f, side, q, 32 + d * c : 32 + d * c + d, :] = v[16:cols]
                return carry

            lax.fori_loop(0, d, body, 0)

        rows_of(0, rows - d)
        rows_of(1, 0)

        def cols_of(i, carry):
            for c in range(2):
                v = own[f, c, i] * scale
                send_cols[f, 0, i, d * c : d * c + d, :] = v[cols - d : cols]
                send_cols[f, 1, i, d * c : d * c + d, :] = v[0:d]
            return carry

        lax.fori_loop(0, rows, cols_of, 0)

        def corners_of(q, carry):
            for k, (si, sj) in enumerate(CORNERS):
                i = q + (rows - 3 if si < 0 else 0)
                send_corn[f, k, q, :, :] = send_cols[f, 0 if sj < 0 else 1, i]
            return carry

        lax.fori_loop(0, 3, corners_of, 0)

    def remote(src, dst, n, to):
        return pltpu.make_async_remote_copy(
            src_ref=src, dst_ref=dst, send_sem=send_sem.at[n], recv_sem=recv_sem.at[n],
            device_id=to, device_id_type=MESH,
        )

    def field_copies(f):
        copies = []
        for k, (si, sj) in enumerate(ROW_SIDES):
            copies.append(remote(send_rows.at[f, k], recv_rows.at[f, k], 8 * f + k, at(-si, -sj)))
        for k, (si, sj) in enumerate(CORNERS):
            copies.append(remote(send_corn.at[f, k], recv_corn.at[f, k], 8 * f + 4 + k, at(-si, -sj)))
        for k, (si, sj) in enumerate(COL_SIDES):
            copies.append(remote(send_cols.at[f, k], recv_cols.at[f, k], 8 * f + 2 + k, at(-si, -sj)))
        return copies

    meta_copies = [
        remote(meta, meta_in.at[k], 16 + k, at(-si, -sj)) for k, (si, sj) in enumerate(SIDES)
    ]
    copies = [field_copies(0), field_copies(1)]

    loads[0].wait()
    pack(0, 1.0)
    pl.semaphore_wait(barrier, len(SIDES) + 1)
    for copy in meta_copies + copies[0]:
        copy.start()
    loads[1].wait()
    pack(1, sign)
    for copy in copies[1]:
        copy.start()

    def place_own(f, dst, scale):
        def body(i, carry):
            for c in range(2):
                fields[dst, c, d + i, 8 : 8 + cols, :] = own[f, c, i] * scale
            return carry

        lax.fori_loop(0, rows, body, 0)

    place_own(0, X0, 1.0)
    place_own(1, L2, sign)

    for copy in meta_copies:
        copy.wait()
    lane = lax.broadcasted_iota(jnp.int32, (3 * rows, 128), 1)

    def widened(west, middle, east):
        w = pltpu.roll(west, 128 - (cols - 8), 1)
        m = pltpu.roll(middle, 8, 1)
        e = pltpu.roll(east, 8 + cols, 1)
        return jnp.where(lane < 8, w, jnp.where(lane < 8 + cols, m, e))

    slot = {side: k for k, side in enumerate(SIDES)}
    for g, si in enumerate((-1, 0, 1)):
        middle = meta[...] if si == 0 else meta_in[slot[si, 0]]
        wide = widened(meta_in[slot[si, -1]], middle, meta_in[slot[si, 1]])
        for p in range(3):
            meta_pad[p, g * rows : (g + 1) * rows, :] = wide[p * rows : (p + 1) * rows]

    which = lax.broadcasted_iota(jnp.int32, (64, 128), 0)
    class_of = (which % 16).astype(jnp.float32)

    def coefficients(r, carry):
        line = pl.ds(rows - d + r, 1)
        mu = meta_pad[2, line, :]
        high = mu.astype(jnp.bfloat16).astype(jnp.float32)
        mid = (mu - high).astype(jnp.bfloat16).astype(jnp.float32)
        low = mu - high - mid
        hot = jnp.where(meta_pad[0, line, :] == class_of, 1.0, 0.0)
        parts = jnp.where(which == 48, high, jnp.where(which == 49, mid, jnp.where(which == 50, low, 0.0)))
        lhs = jnp.where(which < 48, hot, parts).astype(jnp.bfloat16)[:, 0:32]
        dims = (((0,), (0,)), ((), ()))
        got = lax.dot_general(lhs, tab[...], dims, preferred_element_type=jnp.float32)
        for e in range(4):
            cf[1 + e, r] = got[:, e * 128 : e * 128 + 128]
        cf[0, r] = got[:, 512:640]
        hot = jnp.where((meta_pad[1, line, :] == class_of) & (which < 48), 1.0, 0.0)
        lhs = hot.astype(jnp.bfloat16)[:, 0:32]
        got = lax.dot_general(lhs, tab[:, 0:512], dims, preferred_element_type=jnp.float32)
        for e in range(4):
            cf[5 + e, r] = got[:, e * 128 : e * 128 + 128]
        return carry

    lax.fori_loop(0, rows + 2 * d, coefficients, 0)

    def place_halo(f, dst):
        def cols_in(i, carry):
            for c in range(2):
                piece = slice(d * c, d * c + d)
                fields[dst, c, d + i, left0:8, :] = recv_cols[f, 0, i, piece, :]
                fields[dst, c, d + i, 8 + cols : 8 + cols + d, :] = recv_cols[f, 1, i, piece, :]
            return carry

        lax.fori_loop(0, rows, cols_in, 0)

        def rows_in(q, carry):
            for k, base in ((0, 0), (1, d + rows)):
                for c in range(2):
                    fields[dst, c, base + q, 8:24, :] = recv_rows[f, k, q, 16 * c : 16 * c + 16, :]
                    fields[dst, c, base + q, 24 : 8 + cols, :] = recv_rows[
                        f, k, q, 32 + d * c : 32 + d * c + d, :
                    ]
            return carry

        lax.fori_loop(0, d, rows_in, 0)

        def corners_in(q, carry):
            for k, (si, sj) in enumerate(CORNERS):
                r = q + (1 if si < 0 else d + rows)
                first = left0 if sj < 0 else 8 + cols
                for c in range(2):
                    fields[dst, c, r, first : first + d, :] = recv_corn[f, k, q, d * c : d * c + d, :]
            return carry

        lax.fori_loop(0, 3, corners_in, 0)

    def apply(src, first, last, emit):
        def body(r, carry):
            for h in range(halves):
                lanes = slice(h * 128, h * 128 + 128)
                c0, c1 = fields[src, 0, r, :, lanes], fields[src, 1, r, :, lanes]
                d0, d1 = fields[src, 0, r + 1, :, lanes], fields[src, 1, r + 1, :, lanes]
                u0, u1 = fields[src, 0, r - 1, :, lanes], fields[src, 1, r - 1, :, lanes]
                r0, r1 = pltpu.roll(c0, 31, 0), pltpu.roll(c1, 31, 0)
                mu = cf[0, r]
                b = [cf[1 + e, r] for e in range(4)]
                v = [cf[5 + e, r] for e in range(4)]
                p = [cf[5 + e, r - 1] for e in range(4)]
                w0 = mu * c1 + b[0] * r0 + b[1] * r1 + v[0] * d0 + v[1] * d1
                w0 = w0 - (p[0] * u0 + p[2] * u1) - pltpu.roll(b[0] * c0 + b[2] * c1, 1, 0)
                w1 = b[2] * r0 + b[3] * r1 + v[2] * d0 + v[3] * d1 - mu * c0
                w1 = w1 - (p[1] * u0 + p[3] * u1) - pltpu.roll(b[1] * c0 + b[3] * c1, 1, 0)
                emit(r, lanes, (w0, w1))
            return carry

        lax.fori_loop(first, last, body, 0)

    def plus(dst, base, factor):
        def emit(r, lanes, w):
            for c in range(2):
                moved = w[c] + w[c] if factor == 2 else w[c]
                fields[dst, c, r, :, lanes] = fields[base, c, r, :, lanes] + moved
        return emit

    def minus_twice(dst):
        def emit(r, lanes, w):
            for c in range(2):
                fields[dst, c, r, :, lanes] = -2.0 * w[c]
        return emit

    def closing(dst, base, mid):
        def emit(r, lanes, w):
            for c in range(2):
                fields[dst, c, r, :, lanes] = (
                    fields[base, c, r, :, lanes] + fields[mid, c, r, :, lanes] - w[c]
                )
        return emit

    def start_of(r, lanes, w):
        for c in range(2):
            whole = fields[L1, c, r, :, lanes] + fields[LY0, c, r, :, lanes] - w[c]
            out_ref[c, r - d, :, lanes] = whole[8 : 8 + cols]

    end = d + rows
    for copy in copies[0]:
        copy.wait()
    place_halo(0, X0)
    apply(X0, d - 2, end + 3, plus(Y0, X0, 1))
    apply(Y0, d - 1, end + 2, plus(X1, X0, 2))
    apply(X1, d, end + 1, plus(Y1, X1, 1))

    for copy in copies[1]:
        copy.wait()
    place_halo(1, L2)
    apply(L2, d - 3, end + 3, minus_twice(LY1))
    apply(LY1, d - 2, end + 2, closing(L1, L2, LY1))
    apply(L1, d - 1, end + 1, minus_twice(LY0))
    apply(LY0, d, end, start_of)

    own_lines = slice(8, 32)

    def gradient(i, carry):
        r = d + i
        sums = [jnp.zeros((24, 128), jnp.float32) for _ in range(8)]
        for h in range(halves):
            lanes = slice(h * 128, h * 128 + 128)
            for lam, val, twice in ((L2, Y1, True), (LY1, X1, False), (L1, Y0, True), (LY0, X0, False)):
                l = [fields[lam, c, r, own_lines, lanes] for c in range(2)]
                v = [fields[val, c, r, own_lines, lanes] for c in range(2)]
                ld = [fields[lam, c, r + 1, own_lines, lanes] for c in range(2)]
                vd = [fields[val, c, r + 1, own_lines, lanes] for c in range(2)]
                if twice:
                    l = [x + x for x in l]
                    ld = [x + x for x in ld]
                lr = [pltpu.roll(x, 23, 0) for x in l]
                vr = [pltpu.roll(x, 23, 0) for x in v]
                for a in range(2):
                    for b in range(2):
                        e = 2 * a + b
                        sums[e] = sums[e] + (l[a] * vr[b] - v[a] * lr[b])
                        sums[4 + e] = sums[4 + e] + (l[a] * vd[b] - v[a] * ld[b])
        for e in range(8):
            acc[e, i] = half_step * sums[e]
        return carry

    lax.fori_loop(0, rows, gradient, 0)

    total = jnp.zeros((8, 24 * rows), jnp.float32)
    entry = lax.broadcasted_iota(jnp.int32, (8, 128), 0)
    for e in range(8):
        chosen = jnp.where(entry == e, 1.0, 0.0)
        total = total + lax.dot_general(
            chosen, acc[e].reshape(24 * rows, 128), (((1,), (1,)), ((), ())),
            precision=lax.Precision.HIGHEST, preferred_element_type=jnp.float32,
        )
    part[...] = total
    swap = remote(part, part_in, 24, other)
    swap.start()
    swap.wait()
    total = part[...] + part_in[...]
    grad_ref[...] = jnp.where(orb == 0, total[0:4], total[4:8])


def on_device(sizes, checkpoint, cotangent, onsite, bond_class, bond_table, occupied):
    _, _, _, rows, cols, width = sizes
    d = DEPTH
    f32 = jnp.float32
    vmem = pl.BlockSpec(memory_space=pltpu.VMEM)
    hbm = pl.BlockSpec(memory_space=pl.ANY)
    start, grads = pl.pallas_call(
        functools.partial(kernel, sizes),
        out_shape=(
            jax.ShapeDtypeStruct(checkpoint.shape, f32),
            jax.ShapeDtypeStruct((4, 24 * rows), f32),
        ),
        in_specs=[hbm, hbm, vmem, vmem, vmem, vmem],
        out_specs=(vmem, vmem),
        scratch_shapes=[
            pltpu.VMEM((2, 2, rows, cols, width), f32),
            pltpu.VMEM((8, 2, rows + 2 * d, 32, width), f32),
            pltpu.VMEM((9, rows + 2 * d, 32, 128), f32),
            pltpu.VMEM((64, 640), jnp.bfloat16),
            pltpu.VMEM((8, rows, 24, 128), f32),
            pltpu.VMEM((8, 24 * rows), f32),
            pltpu.VMEM((8, 24 * rows), f32),
            pltpu.VMEM((2, 2, d, 2 * cols, width), f32),
            pltpu.VMEM((2, 2, d, 2 * cols, width), f32),
            pltpu.VMEM((2, 2, rows, 2 * d, width), f32),
            pltpu.VMEM((2, 2, rows, 2 * d, width), f32),
            pltpu.VMEM((2, 4, 3, 2 * d, width), f32),
            pltpu.VMEM((2, 4, 3, 2 * d, width), f32),
            pltpu.VMEM((3 * rows, 128), f32),
            pltpu.VMEM((8, 3 * rows, 128), f32),
            pltpu.VMEM((3, 3 * rows, 128), f32),
            pltpu.SemaphoreType.DMA((2,)),
            pltpu.SemaphoreType.DMA((25,)),
            pltpu.SemaphoreType.DMA((25,)),
        ],
        compiler_params=pltpu.CompilerParams(
            collective_id=0, has_side_effects=True, vmem_limit_bytes=40 * 1024 * 1024
        ),
        cost_estimate=pl.CostEstimate(flops=60_000_000, bytes_accessed=1_500_000, transcendentals=0),
    )(checkpoint, cotangent, onsite, bond_class, bond_table, occupied.reshape(1, width))
    return start, grads.reshape(4, rows, 24)[:, :, :cols]


def solution(mesh):
    shape = mesh.shape

    def body(checkpoint, cotangent, onsite, bond_class, bond_table, occupied):
        _, rows, cols, width = checkpoint.shape
        sizes = (shape["gy"], shape["gx"], shape["orb"], rows, cols, width)
        return on_device(sizes, checkpoint, cotangent, onsite, bond_class, bond_table, occupied)

    in_specs = (
        P("groups", "gy", "gx", "orb"),
        P("groups", "gy", "gx", "orb"),
        P(("groups", "gy"), "gx"),
        P("groups", "gy", "gx"),
        P(),
        P(("groups", "orb")),
    )
    out_specs = (P("groups", "gy", "gx", "orb"), P(("groups", "orb"), "gy", "gx"))
    return jax.shard_map(body, mesh=mesh, in_specs=in_specs, out_specs=out_specs, check_vma=False)
```

```python
import functools

import jax
import jax.numpy as jnp
from jax import lax
from jax.experimental import pallas as pl
from jax.experimental.pallas import tpu as pltpu
from jax.sharding import PartitionSpec as P

half_step = 0.05
DEPTH = 4
MESH = pl.DeviceIdType.MESH
SIDES = ((-1, 0), (1, 0), (0, -1), (0, 1))
X0, Y0, X1, Y1, L2, LY1, L1, LY0 = range(8)


def kernel(
    sizes, x_hbm, c_hbm, onsite_ref, class_ref, table_ref, occ_ref,
    out_ref, grad_ref,
    own, fields, cf, tab, hot_ref, acc, part, part_in,
    send_rows, recv_rows, meta, meta_in, meta_mid, meta_side, meta_pad,
    copy_sem, send_sem, recv_sem,
):
    gy_n, gx_n, orb_n, rows, cols, width = sizes
    halves = width // 128
    gy, gx, orb = lax.axis_index("gy"), lax.axis_index("gx"), lax.axis_index("orb")
    d = DEPTH
    end = d + cols
    wide_cols = cols + 2 * d

    def at(si, sj):
        return {
            "gy": lax.rem(gy + si + gy_n, gy_n),
            "gx": lax.rem(gx + sj + gx_n, gx_n),
        }

    other_orb = lax.rem(orb + 1, orb_n)
    other = {"orb": other_orb}

    load_c = pltpu.make_async_copy(c_hbm, own, copy_sem.at[0])
    load_x = pltpu.make_async_copy(x_hbm, fields.at[X0, :, d:end, 0:8, :], copy_sem.at[1])
    load_c.start()
    load_x.start()

    barrier = pltpu.get_barrier_semaphore()
    for si, sj in SIDES:
        pl.semaphore_signal(barrier, inc=1, device_id=at(si, sj), device_id_type=MESH)
    pl.semaphore_signal(barrier, inc=1, device_id=other, device_id_type=MESH)

    meta[0:rows, 0:cols] = class_ref[0].astype(jnp.float32)
    meta[rows : 2 * rows, 0:cols] = class_ref[1].astype(jnp.float32)
    meta[2 * rows : 3 * rows, 0:cols] = half_step * onsite_ref[...]

    upper = lax.broadcasted_iota(jnp.int32, (8, width), 0) < 4

    def pack(f, j, c0, c1):
        turned = pltpu.roll(c1, 4, 0)
        send_rows[f, 0, j] = jnp.where(upper, c0, turned)
        send_rows[f, 1, j] = jnp.where(upper, turned, c0)

    def pack_c(j, carry):
        sign = (2 * occ_ref[...] - 1).astype(jnp.float32)
        c0, c1 = own[0, j] * sign, own[1, j] * sign
        fields[L2, 0, d + j, 0:8, :] = c0
        fields[L2, 1, d + j, 0:8, :] = c1
        pack(1, j, c0, c1)
        return carry

    def pack_x(j, carry):
        pack(0, j, fields[X0, 0, d + j, 0:8, :], fields[X0, 1, d + j, 0:8, :])
        return carry

    def remote(src, dst, n, to):
        return pltpu.make_async_remote_copy(
            src_ref=src, dst_ref=dst, send_sem=send_sem.at[n], recv_sem=recv_sem.at[n],
            device_id=to, device_id_type=MESH,
        )

    def field_copies(f, name):
        copies = []
        for k, si in ((0, 1), (1, -1)):
            copies.append(
                remote(send_rows.at[f, k], recv_rows.at[f, k, d:end], 8 * f + k, at(-si, 0))
            )
        mine = fields.at[name]
        copies.append(remote(
            mine.at[:, cols:end, 0:8, :], mine.at[:, 0:d, 0:8, :], 8 * f + 6, at(0, 1)
        ))
        copies.append(remote(
            mine.at[:, d : 2 * d, 0:8, :], mine.at[:, end : end + d, 0:8, :], 8 * f + 7, at(0, -1)
        ))
        return copies

    def corner_copies(f, k):
        got = recv_rows.at[f, k]
        return [
            remote(got.at[cols + 1 : end], got.at[1:d], 8 * f + 2 + k, at(0, 1)),
            remote(got.at[d : d + 3], got.at[end : end + 3], 8 * f + 4 + k, at(0, -1)),
        ]

    meta_copies = [
        remote(meta, meta_in.at[k], 16 + k, at(*to)) for k, to in enumerate(SIDES[:2])
    ]
    meta_wide = [
        remote(meta_mid, meta_side.at[k], 18 + k, at(*to)) for k, to in enumerate(SIDES[2:])
    ]
    copies_x, copies_c = field_copies(0, X0), field_copies(1, L2)

    load_c.wait()
    lax.fori_loop(0, cols, pack_c, 0)
    pl.semaphore_wait(barrier, len(SIDES) + 1)
    for copy in meta_copies + copies_c:
        copy.start()
    load_x.wait()
    lax.fori_loop(0, cols, pack_x, 0)
    for copy in copies_x:
        copy.start()

    diagonal = lax.broadcasted_iota(jnp.int32, (16, 16), 0) == lax.broadcasted_iota(
        jnp.int32, (16, 16), 1
    )
    blank = jnp.zeros((16, 128), jnp.bfloat16)
    for e in range(4):
        column = jnp.sum(jnp.where(diagonal, table_ref[e : e + 1, :], 0.0), axis=1, keepdims=True)
        t = jnp.broadcast_to(half_step * column, (16, 128))
        high = t.astype(jnp.bfloat16)
        rest = t - high.astype(jnp.float32)
        mid = rest.astype(jnp.bfloat16)
        lanes = slice(e * 128, e * 128 + 128)
        tab[0:16, lanes] = high
        tab[16:32, lanes] = mid
        tab[32:48, lanes] = (rest - mid.astype(jnp.float32)).astype(jnp.bfloat16)
        tab[48:64, lanes] = blank
    for n in range(3):
        tab[16 * n : 16 * n + 16, 512:640] = blank
    tab[48:64, 512:640] = jnp.ones((16, 128), jnp.bfloat16)

    for copy in meta_copies:
        copy.wait()
    upper_tile = lax.broadcasted_iota(jnp.int32, (8, 128), 0) < 4
    for p in range(3):
        of = slice(p * rows, (p + 1) * rows)
        meta_mid[p, 0:8, :] = meta[of]
        meta_mid[p, 8:16, :] = jnp.where(upper_tile, meta_in[0, of], meta_in[1, of])
    for copy in meta_wide:
        copy.start()
    for copy in meta_wide:
        copy.wait()
    lane = lax.broadcasted_iota(jnp.int32, (16, 128), 1)
    for p in range(3):
        west = pltpu.roll(meta_side[1, p], 128 - (cols - d), 1)
        east = pltpu.roll(meta_side[0, p], end, 1)
        middle = pltpu.roll(meta_mid[p], d, 1)
        meta_pad[p] = jnp.where(lane < d, west, jnp.where(lane < end, middle, east))

    which = lax.broadcasted_iota(jnp.int32, (16, 64), 1)
    class_of = (which % 16).astype(jnp.float32)
    for j in range(wide_cols):
        lines = slice(16 * j, 16 * j + 16)
        mu = meta_pad[2, :, j : j + 1]
        high = mu.astype(jnp.bfloat16).astype(jnp.float32)
        mid = (mu - high).astype(jnp.bfloat16).astype(jnp.float32)
        low = mu - high - mid
        hot = jnp.where(meta_pad[0, :, j : j + 1] == class_of, 1.0, 0.0)
        parts = jnp.where(
            which == 48, high, jnp.where(which == 49, mid, jnp.where(which == 50, low, 0.0))
        )
        hot_ref[0, lines, :] = jnp.where(which < 48, hot, parts).astype(jnp.bfloat16)
        hot = jnp.where((meta_pad[1, :, j : j + 1] == class_of) & (which < 48), 1.0, 0.0)
        hot_ref[1, lines, :] = hot.astype(jnp.bfloat16)

    def coefficients(q, carry):
        lines = pl.ds(pl.multiple_of(64 * q, 64), 64)
        got = jnp.dot(hot_ref[0, lines, :], tab[...], preferred_element_type=jnp.float32)
        for e in range(4):
            cf[1 + e, pl.ds(4 * q, 4)] = got[:, e * 128 : e * 128 + 128].reshape(4, 16, 128)
        cf[0, pl.ds(4 * q, 4)] = got[:, 512:640].reshape(4, 16, 128)
        got = jnp.dot(hot_ref[1, lines, :], tab[:, 0:512], preferred_element_type=jnp.float32)
        for e in range(4):
            cf[5 + e, pl.ds(4 * q, 4)] = got[:, e * 128 : e * 128 + 128].reshape(4, 16, 128)
        return carry

    lax.fori_loop(0, wide_cols // 4, coefficients, 0)

    def place_halo(f, name, first, last):
        def body(j, carry):
            below, above = recv_rows[f, 0, j], recv_rows[f, 1, j]
            fields[name, 0, j, 8:16, :] = jnp.where(upper, below, above)
            fields[name, 1, j, 8:16, :] = pltpu.roll(jnp.where(upper, above, below), 4, 0)
            return carry

        lax.fori_loop(first, last, body, 0)

    def apply(src, first, last, emit):
        def body(j, carry):
            for h in range(halves):
                lanes = slice(h * 128, h * 128 + 128)
                c0, c1 = fields[src, 0, j, :, lanes], fields[src, 1, j, :, lanes]
                r0, r1 = fields[src, 0, j + 1, :, lanes], fields[src, 1, j + 1, :, lanes]
                l0, l1 = fields[src, 0, j - 1, :, lanes], fields[src, 1, j - 1, :, lanes]
                d0, d1 = pltpu.roll(c0, 15, 0), pltpu.roll(c1, 15, 0)
                mu = cf[0, j]
                b = [cf[1 + e, j] for e in range(4)]
                p = [cf[1 + e, j - 1] for e in range(4)]
                v = [cf[5 + e, j] for e in range(4)]
                w0 = mu * c1 + b[0] * r0 + b[1] * r1 + v[0] * d0 + v[1] * d1
                w0 = w0 - (p[0] * l0 + p[2] * l1) - pltpu.roll(v[0] * c0 + v[2] * c1, 1, 0)
                w1 = b[2] * r0 + b[3] * r1 + v[2] * d0 + v[3] * d1 - mu * c0
                w1 = w1 - (p[1] * l0 + p[3] * l1) - pltpu.roll(v[1] * c0 + v[3] * c1, 1, 0)
                emit(j, lanes, (w0, w1))
            return carry

        lax.fori_loop(first, last, body, 0)

    def plus(dst, base, factor):
        def emit(j, lanes, w):
            for c in range(2):
                moved = w[c] + w[c] if factor == 2 else w[c]
                fields[dst, c, j, :, lanes] = fields[base, c, j, :, lanes] + moved
        return emit

    def minus_twice(dst):
        def emit(j, lanes, w):
            for c in range(2):
                fields[dst, c, j, :, lanes] = -2.0 * w[c]
        return emit

    def closing(dst, base, mid):
        def emit(j, lanes, w):
            for c in range(2):
                fields[dst, c, j, :, lanes] = (
                    fields[base, c, j, :, lanes] + fields[mid, c, j, :, lanes] - w[c]
                )
        return emit

    def start_of(j, lanes, w):
        for c in range(2):
            out_ref[c, j - d, :, lanes] = (
                fields[L1, c, j, 0:8, lanes] + fields[LY0, c, j, 0:8, lanes] - w[c][0:8]
            )

    def arrive(f, name, copies, step):
        corners = []
        for k in range(2):
            copies[k].wait_recv()
            sent = corner_copies(f, k)
            for copy in sent:
                copy.start()
            corners += sent
        place_halo(f, name, d, end)
        apply(name, d + 1, end - 1, step)
        for copy in copies[2:] + corners:
            copy.wait_recv()
        place_halo(f, name, 1, d)
        place_halo(f, name, end, end + 3)
        return corners

    step = minus_twice(LY1)
    corners_c = arrive(1, L2, copies_c, step)
    apply(L2, d - 3, d + 1, step)
    apply(L2, end - 1, end + 3, step)
    apply(LY1, d - 2, end + 2, closing(L1, L2, LY1))
    apply(L1, d - 1, end + 1, minus_twice(LY0))
    apply(LY0, d, end, start_of)

    step = plus(Y0, X0, 1)
    corners_x = arrive(0, X0, copies_x, step)
    apply(X0, d - 2, d + 1, step)
    apply(X0, end - 1, end + 3, step)
    apply(Y0, d - 1, end + 2, plus(X1, X0, 2))
    apply(X1, d, end + 1, plus(Y1, X1, 1))
    for copy in copies_c + corners_c + copies_x + corners_x:
        copy.wait_send()

    def gradient(i, carry):
        j = d + i
        sums = [jnp.zeros((8, 128), jnp.float32) for _ in range(8)]
        for h in range(halves):
            lanes = slice(h * 128, h * 128 + 128)
            for lam, val, twice in (
                (L2, Y1, True), (LY1, X1, False), (L1, Y0, True), (LY0, X0, False)
            ):
                l = [fields[lam, c, j, 0:8, lanes] for c in range(2)]
                v = [fields[val, c, j, 0:8, lanes] for c in range(2)]
                ld = [fields[lam, c, j, 1:9, lanes] for c in range(2)]
                vd = [fields[val, c, j, 1:9, lanes] for c in range(2)]
                lr = [fields[lam, c, j + 1, 0:8, lanes] for c in range(2)]
                vr = [fields[val, c, j + 1, 0:8, lanes] for c in range(2)]
                if twice:
                    v, vd, vr = ([x + x for x in group] for group in (v, vd, vr))
                for a in range(2):
                    for b in range(2):
                        e = 2 * a + b
                        sums[e] = sums[e] + (l[a] * vr[b] - v[a] * lr[b])
                        sums[4 + e] = sums[4 + e] + (l[a] * vd[b] - v[a] * ld[b])
        for e in range(8):
            acc[e, i] = sums[e]
        return carry

    lax.fori_loop(0, cols, gradient, 0)

    place = lax.broadcasted_iota(jnp.int32, (8, 128), 1)
    for e in range(8):
        total = jnp.zeros((8, 128), jnp.float32)
        for j in range(cols):
            total = jnp.where(place == j, jnp.sum(acc[e, j], axis=1, keepdims=True), total)
        part[e] = half_step * total
    swap = remote(part.at[pl.ds(4 * other_orb, 4)], part_in, 24, other)
    swap.start()
    swap.wait()
    total = part[pl.ds(4 * orb, 4)] + part_in[...]
    grad_ref[...] = total[:, :, 0:cols]


def on_device(sizes, checkpoint, cotangent, onsite, bond_class, bond_table, occupied):
    _, _, _, rows, cols, width = sizes
    d = DEPTH
    f32 = jnp.float32
    vmem = pl.BlockSpec(memory_space=pltpu.VMEM)
    hbm = pl.BlockSpec(memory_space=pl.ANY)
    start, grads = pl.pallas_call(
        functools.partial(kernel, sizes),
        out_shape=(
            jax.ShapeDtypeStruct((2, cols, rows, width), f32),
            jax.ShapeDtypeStruct((4, rows, cols), f32),
        ),
        in_specs=[hbm, hbm, vmem, vmem, vmem, vmem],
        out_specs=(vmem, vmem),
        scratch_shapes=[
            pltpu.VMEM((2, cols, rows, width), f32),
            pltpu.VMEM((8, 2, cols + 2 * d, 16, width), f32),
            pltpu.VMEM((9, cols + 2 * d, 16, 128), f32),
            pltpu.VMEM((64, 640), jnp.bfloat16),
            pltpu.VMEM((2, 16 * (cols + 2 * d), 64), jnp.bfloat16),
            pltpu.VMEM((8, cols, 8, 128), f32),
            pltpu.VMEM((8, 8, 128), f32),
            pltpu.VMEM((4, 8, 128), f32),
            pltpu.VMEM((2, 2, cols, 8, width), f32),
            pltpu.VMEM((2, 2, cols + 2 * d, 8, width), f32),
            pltpu.VMEM((3 * rows, 128), f32),
            pltpu.VMEM((2, 3 * rows, 128), f32),
            pltpu.VMEM((3, 16, 128), f32),
            pltpu.VMEM((2, 3, 16, 128), f32),
            pltpu.VMEM((3, 16, 128), f32),
            pltpu.SemaphoreType.DMA((2,)),
            pltpu.SemaphoreType.DMA((25,)),
            pltpu.SemaphoreType.DMA((25,)),
        ],
        compiler_params=pltpu.CompilerParams(
            collective_id=0, has_side_effects=True, vmem_limit_bytes=40 * 1024 * 1024
        ),
        cost_estimate=pl.CostEstimate(flops=60_000_000, bytes_accessed=1_500_000, transcendentals=0),
    )(
        checkpoint.transpose(0, 2, 1, 3), cotangent.transpose(0, 2, 1, 3), onsite, bond_class,
        bond_table.T, occupied.reshape(1, width),
    )
    return start.transpose(0, 2, 1, 3), grads


def solution(mesh):
    shape = mesh.shape

    def body(checkpoint, cotangent, onsite, bond_class, bond_table, occupied):
        _, rows, cols, width = checkpoint.shape
        sizes = (shape["gy"], shape["gx"], shape["orb"], rows, cols, width)
        return on_device(sizes, checkpoint, cotangent, onsite, bond_class, bond_table, occupied)

    in_specs = (
        P("groups", "gy", "gx", "orb"),
        P("groups", "gy", "gx", "orb"),
        P(("groups", "gy"), "gx"),
        P("groups", "gy", "gx"),
        P(),
        P(("groups", "orb")),
    )
    out_specs = (P("groups", "gy", "gx", "orb"), P(("groups", "orb"), "gy", "gx"))
    return jax.shard_map(body, mesh=mesh, in_specs=in_specs, out_specs=out_specs, check_vma=False)
```

```python
import functools

import jax
import jax.numpy as jnp
from jax import lax
from jax.experimental import pallas as pl
from jax.experimental.pallas import tpu as pltpu
from jax.sharding import PartitionSpec as P

half_step = 0.05
DEPTH = 4
ROW_SEM = 25
MESH = pl.DeviceIdType.MESH
SIDES = ((-1, 0), (1, 0), (0, -1), (0, 1))
X0, Y0, X1, Y1, L2, LY1, L1, LY0 = range(8)


def kernel(
    sizes, x_hbm, c_hbm, onsite_ref, class_ref, table_ref, occ_ref,
    out_ref, grad_ref,
    own, fields, cf, tab, hot_ref, acc, part, part_in,
    send_rows, recv_rows, meta, meta_in, meta_mid, meta_side, meta_pad,
    copy_sem, send_sem, recv_sem,
):
    gy_n, gx_n, orb_n, rows, cols, width = sizes
    halves = width // 128
    gy, gx, orb = lax.axis_index("gy"), lax.axis_index("gx"), lax.axis_index("orb")
    d = DEPTH
    end = d + cols
    wide_cols = cols + 2 * d

    def at(si, sj):
        return {
            "gy": lax.rem(gy + si + gy_n, gy_n),
            "gx": lax.rem(gx + sj + gx_n, gx_n),
        }

    other_orb = lax.rem(orb + 1, orb_n)
    other = {"orb": other_orb}

    load_c = pltpu.make_async_copy(c_hbm, own, copy_sem.at[0])
    load_x = pltpu.make_async_copy(x_hbm, fields.at[X0, :, d:end, 0:8, :], copy_sem.at[1])
    load_c.start()
    load_x.start()

    barrier = pltpu.get_barrier_semaphore()
    for si, sj in SIDES:
        pl.semaphore_signal(barrier, inc=1, device_id=at(si, sj), device_id_type=MESH)
    pl.semaphore_signal(barrier, inc=1, device_id=other, device_id_type=MESH)

    meta[0:rows, 0:cols] = class_ref[0].astype(jnp.float32)
    meta[rows : 2 * rows, 0:cols] = class_ref[1].astype(jnp.float32)
    meta[2 * rows : 3 * rows, 0:cols] = half_step * onsite_ref[...]

    upper = lax.broadcasted_iota(jnp.int32, (8, width), 0) < 4

    def pack(f, j, c0, c1):
        turned = pltpu.roll(c1, 4, 0)
        send_rows[f, 0, j] = jnp.where(upper, c0, turned)
        send_rows[f, 1, j] = jnp.where(upper, turned, c0)

    def pack_c(j, carry):
        sign = (2 * occ_ref[...] - 1).astype(jnp.float32)
        c0, c1 = own[0, j] * sign, own[1, j] * sign
        fields[L2, 0, d + j, 0:8, :] = c0
        fields[L2, 1, d + j, 0:8, :] = c1
        pack(1, j, c0, c1)
        return carry

    def pack_x(j, carry):
        pack(0, j, fields[X0, 0, d + j, 0:8, :], fields[X0, 1, d + j, 0:8, :])
        return carry

    def remote(src, dst, n, to):
        return pltpu.make_async_remote_copy(
            src_ref=src, dst_ref=dst, send_sem=send_sem.at[n], recv_sem=recv_sem.at[n],
            device_id=to, device_id_type=MESH,
        )

    def field_copies(f, name):
        edges, copies = [], []
        for k, si in ((0, 1), (1, -1)):
            for n, (first, last) in enumerate(((0, 3), (cols - 3, cols), (3, cols - 3))):
                copy = remote(
                    send_rows.at[f, k, first:last], recv_rows.at[f, k, d + first : d + last],
                    ROW_SEM + 6 * f + 3 * k + n, at(-si, 0),
                )
                (edges if n < 2 else copies).append(copy)
        mine = fields.at[name]
        copies.append(remote(
            mine.at[:, cols:end, 0:8, :], mine.at[:, 0:d, 0:8, :], 8 * f + 6, at(0, 1)
        ))
        copies.append(remote(
            mine.at[:, d : 2 * d, 0:8, :], mine.at[:, end : end + d, 0:8, :], 8 * f + 7, at(0, -1)
        ))
        return edges, copies

    def corner_copies(f, k):
        got = recv_rows.at[f, k]
        return [
            remote(got.at[cols + 1 : end], got.at[1:d], 8 * f + 2 + k, at(0, 1)),
            remote(got.at[d : d + 3], got.at[end : end + 3], 8 * f + 4 + k, at(0, -1)),
        ]

    meta_copies = [
        remote(meta, meta_in.at[k], 16 + k, at(*to)) for k, to in enumerate(SIDES[:2])
    ]
    meta_wide = [
        remote(meta_mid, meta_side.at[k], 18 + k, at(*to)) for k, to in enumerate(SIDES[2:])
    ]
    (edges_x, copies_x), (edges_c, copies_c) = field_copies(0, X0), field_copies(1, L2)

    load_c.wait()
    lax.fori_loop(0, cols, pack_c, 0)
    pl.semaphore_wait(barrier, len(SIDES) + 1)
    for copy in meta_copies + edges_c:
        copy.start()
    load_x.wait()
    lax.fori_loop(0, cols, pack_x, 0)
    for copy in edges_x + copies_c + copies_x:
        copy.start()

    diagonal = lax.broadcasted_iota(jnp.int32, (16, 16), 0) == lax.broadcasted_iota(
        jnp.int32, (16, 16), 1
    )
    blank = jnp.zeros((16, 128), jnp.bfloat16)
    for e in range(4):
        column = jnp.sum(jnp.where(diagonal, table_ref[e : e + 1, :], 0.0), axis=1, keepdims=True)
        t = jnp.broadcast_to(half_step * column, (16, 128))
        high = t.astype(jnp.bfloat16)
        rest = t - high.astype(jnp.float32)
        mid = rest.astype(jnp.bfloat16)
        lanes = slice(e * 128, e * 128 + 128)
        tab[0:16, lanes] = high
        tab[16:32, lanes] = mid
        tab[32:48, lanes] = (rest - mid.astype(jnp.float32)).astype(jnp.bfloat16)
        tab[48:64, lanes] = blank
    for n in range(3):
        tab[16 * n : 16 * n + 16, 512:640] = blank
    tab[48:64, 512:640] = jnp.ones((16, 128), jnp.bfloat16)

    for copy in meta_copies:
        copy.wait()
    upper_tile = lax.broadcasted_iota(jnp.int32, (8, 128), 0) < 4
    for p in range(3):
        of = slice(p * rows, (p + 1) * rows)
        meta_mid[p, 0:8, :] = meta[of]
        meta_mid[p, 8:16, :] = jnp.where(upper_tile, meta_in[0, of], meta_in[1, of])
    for copy in meta_wide:
        copy.start()
    for copy in meta_wide:
        copy.wait()
    lane = lax.broadcasted_iota(jnp.int32, (16, 128), 1)
    for p in range(3):
        west = pltpu.roll(meta_side[1, p], 128 - (cols - d), 1)
        east = pltpu.roll(meta_side[0, p], end, 1)
        middle = pltpu.roll(meta_mid[p], d, 1)
        meta_pad[p] = jnp.where(lane < d, west, jnp.where(lane < end, middle, east))

    which = lax.broadcasted_iota(jnp.int32, (16, 64), 1)
    class_of = (which % 16).astype(jnp.float32)
    for j in range(wide_cols):
        lines = slice(16 * j, 16 * j + 16)
        mu = meta_pad[2, :, j : j + 1]
        high = mu.astype(jnp.bfloat16).astype(jnp.float32)
        mid = (mu - high).astype(jnp.bfloat16).astype(jnp.float32)
        low = mu - high - mid
        hot = jnp.where(meta_pad[0, :, j : j + 1] == class_of, 1.0, 0.0)
        parts = jnp.where(
            which == 48, high, jnp.where(which == 49, mid, jnp.where(which == 50, low, 0.0))
        )
        hot_ref[0, lines, :] = jnp.where(which < 48, hot, parts).astype(jnp.bfloat16)
        hot = jnp.where((meta_pad[1, :, j : j + 1] == class_of) & (which < 48), 1.0, 0.0)
        hot_ref[1, lines, :] = hot.astype(jnp.bfloat16)

    def coefficients(q, carry):
        lines = pl.ds(pl.multiple_of(64 * q, 64), 64)
        got = jnp.dot(hot_ref[0, lines, :], tab[...], preferred_element_type=jnp.float32)
        for e in range(4):
            cf[1 + e, pl.ds(4 * q, 4)] = got[:, e * 128 : e * 128 + 128].reshape(4, 16, 128)
        cf[0, pl.ds(4 * q, 4)] = got[:, 512:640].reshape(4, 16, 128)
        got = jnp.dot(hot_ref[1, lines, :], tab[:, 0:512], preferred_element_type=jnp.float32)
        for e in range(4):
            cf[5 + e, pl.ds(4 * q, 4)] = got[:, e * 128 : e * 128 + 128].reshape(4, 16, 128)
        return carry

    lax.fori_loop(0, wide_cols // 4, coefficients, 0)

    def place_halo(f, name, first, last):
        def body(j, carry):
            below, above = recv_rows[f, 0, j], recv_rows[f, 1, j]
            fields[name, 0, j, 8:16, :] = jnp.where(upper, below, above)
            fields[name, 1, j, 8:16, :] = pltpu.roll(jnp.where(upper, above, below), 4, 0)
            return carry

        lax.fori_loop(first, last, body, 0)

    def apply(src, first, last, emit):
        def body(j, carry):
            for h in range(halves):
                lanes = slice(h * 128, h * 128 + 128)
                c0, c1 = fields[src, 0, j, :, lanes], fields[src, 1, j, :, lanes]
                r0, r1 = fields[src, 0, j + 1, :, lanes], fields[src, 1, j + 1, :, lanes]
                l0, l1 = fields[src, 0, j - 1, :, lanes], fields[src, 1, j - 1, :, lanes]
                d0, d1 = pltpu.roll(c0, 15, 0), pltpu.roll(c1, 15, 0)
                mu = cf[0, j]
                b = [cf[1 + e, j] for e in range(4)]
                p = [cf[1 + e, j - 1] for e in range(4)]
                v = [cf[5 + e, j] for e in range(4)]
                w0 = mu * c1 + b[0] * r0 + b[1] * r1 + v[0] * d0 + v[1] * d1
                w0 = w0 - (p[0] * l0 + p[2] * l1) - pltpu.roll(v[0] * c0 + v[2] * c1, 1, 0)
                w1 = b[2] * r0 + b[3] * r1 + v[2] * d0 + v[3] * d1 - mu * c0
                w1 = w1 - (p[1] * l0 + p[3] * l1) - pltpu.roll(v[1] * c0 + v[3] * c1, 1, 0)
                emit(j, lanes, (w0, w1))
            return carry

        lax.fori_loop(first, last, body, 0)

    def plus(dst, base, factor):
        def emit(j, lanes, w):
            for c in range(2):
                moved = w[c] + w[c] if factor == 2 else w[c]
                fields[dst, c, j, :, lanes] = fields[base, c, j, :, lanes] + moved
        return emit

    def minus_twice(dst):
        def emit(j, lanes, w):
            for c in range(2):
                fields[dst, c, j, :, lanes] = -2.0 * w[c]
        return emit

    def closing(dst, base, mid):
        def emit(j, lanes, w):
            for c in range(2):
                fields[dst, c, j, :, lanes] = (
                    fields[base, c, j, :, lanes] + fields[mid, c, j, :, lanes] - w[c]
                )
        return emit

    def start_of(j, lanes, w):
        for c in range(2):
            out_ref[c, j - d, :, lanes] = (
                fields[L1, c, j, 0:8, lanes] + fields[LY0, c, j, 0:8, lanes] - w[c][0:8]
            )

    def forward(f, edges):
        corners = []
        for k in range(2):
            for copy in edges[2 * k : 2 * k + 2]:
                copy.wait_recv()
            sent = corner_copies(f, k)
            for copy in sent:
                copy.start()
            corners += sent
        return corners

    corners_c = forward(1, edges_c)
    corners_x = forward(0, edges_x)

    def arrive(f, name, copies, corners):
        for copy in corners + copies:
            copy.wait_recv()
        place_halo(f, name, 1, wide_cols - 1)

    arrive(1, L2, copies_c, corners_c)
    apply(L2, d - 3, end + 3, minus_twice(LY1))
    apply(LY1, d - 2, end + 2, closing(L1, L2, LY1))
    apply(L1, d - 1, end + 1, minus_twice(LY0))
    apply(LY0, d, end, start_of)

    arrive(0, X0, copies_x, corners_x)
    apply(X0, d - 2, end + 3, plus(Y0, X0, 1))
    apply(Y0, d - 1, end + 2, plus(X1, X0, 2))
    apply(X1, d, end + 1, plus(Y1, X1, 1))
    for copy in edges_c + copies_c + corners_c + edges_x + copies_x + corners_x:
        copy.wait_send()

    def gradient(i, carry):
        j = d + i
        sums = [jnp.zeros((8, 128), jnp.float32) for _ in range(8)]
        for h in range(halves):
            lanes = slice(h * 128, h * 128 + 128)
            for lam, val, twice in (
                (L2, Y1, True), (LY1, X1, False), (L1, Y0, True), (LY0, X0, False)
            ):
                l = [fields[lam, c, j, 0:8, lanes] for c in range(2)]
                v = [fields[val, c, j, 0:8, lanes] for c in range(2)]
                ld = [fields[lam, c, j, 1:9, lanes] for c in range(2)]
                vd = [fields[val, c, j, 1:9, lanes] for c in range(2)]
                lr = [fields[lam, c, j + 1, 0:8, lanes] for c in range(2)]
                vr = [fields[val, c, j + 1, 0:8, lanes] for c in range(2)]
                if twice:
                    v, vd, vr = ([x + x for x in group] for group in (v, vd, vr))
                for a in range(2):
                    for b in range(2):
                        e = 2 * a + b
                        sums[e] = sums[e] + (l[a] * vr[b] - v[a] * lr[b])
                        sums[4 + e] = sums[4 + e] + (l[a] * vd[b] - v[a] * ld[b])
        for e in range(8):
            acc[e, i] = sums[e]
        return carry

    lax.fori_loop(0, cols, gradient, 0)

    place = lax.broadcasted_iota(jnp.int32, (8, 128), 1)
    for e in range(8):
        total = jnp.zeros((8, 128), jnp.float32)
        for j in range(cols):
            total = jnp.where(place == j, jnp.sum(acc[e, j], axis=1, keepdims=True), total)
        part[e] = half_step * total
    swap = remote(part.at[pl.ds(4 * other_orb, 4)], part_in, 24, other)
    swap.start()
    swap.wait()
    total = part[pl.ds(4 * orb, 4)] + part_in[...]
    grad_ref[...] = total[:, :, 0:cols]


def on_device(sizes, checkpoint, cotangent, onsite, bond_class, bond_table, occupied):
    _, _, _, rows, cols, width = sizes
    d = DEPTH
    f32 = jnp.float32
    vmem = pl.BlockSpec(memory_space=pltpu.VMEM)
    hbm = pl.BlockSpec(memory_space=pltpu.HBM)
    start, grads = pl.pallas_call(
        functools.partial(kernel, sizes),
        out_shape=(
            jax.ShapeDtypeStruct((2, cols, rows, width), f32),
            jax.ShapeDtypeStruct((4, rows, cols), f32),
        ),
        in_specs=[hbm, hbm, vmem, vmem, vmem, vmem],
        out_specs=(vmem, vmem),
        scratch_shapes=[
            pltpu.VMEM((2, cols, rows, width), f32),
            pltpu.VMEM((8, 2, cols + 2 * d, 16, width), f32),
            pltpu.VMEM((9, cols + 2 * d, 16, 128), f32),
            pltpu.VMEM((64, 640), jnp.bfloat16),
            pltpu.VMEM((2, 16 * (cols + 2 * d), 64), jnp.bfloat16),
            pltpu.VMEM((8, cols, 8, 128), f32),
            pltpu.VMEM((8, 8, 128), f32),
            pltpu.VMEM((4, 8, 128), f32),
            pltpu.VMEM((2, 2, cols, 8, width), f32),
            pltpu.VMEM((2, 2, cols + 2 * d, 8, width), f32),
            pltpu.VMEM((3 * rows, 128), f32),
            pltpu.VMEM((2, 3 * rows, 128), f32),
            pltpu.VMEM((3, 16, 128), f32),
            pltpu.VMEM((2, 3, 16, 128), f32),
            pltpu.VMEM((3, 16, 128), f32),
            pltpu.SemaphoreType.DMA((2,)),
            pltpu.SemaphoreType.DMA((ROW_SEM + 12,)),
            pltpu.SemaphoreType.DMA((ROW_SEM + 12,)),
        ],
        compiler_params=pltpu.CompilerParams(
            collective_id=0, has_side_effects=True, vmem_limit_bytes=40 * 1024 * 1024
        ),
        cost_estimate=pl.CostEstimate(flops=60_000_000, bytes_accessed=1_500_000, transcendentals=0),
    )(
        checkpoint.transpose(0, 2, 1, 3), cotangent.transpose(0, 2, 1, 3), onsite, bond_class,
        bond_table.T, occupied.reshape(1, width),
    )
    return start.transpose(0, 2, 1, 3), grads


def solution(mesh):
    shape = mesh.shape

    def body(checkpoint, cotangent, onsite, bond_class, bond_table, occupied):
        _, rows, cols, width = checkpoint.shape
        sizes = (shape["gy"], shape["gx"], shape["orb"], rows, cols, width)
        return on_device(sizes, checkpoint, cotangent, onsite, bond_class, bond_table, occupied)

    in_specs = (
        P("groups", "gy", "gx", "orb"),
        P("groups", "gy", "gx", "orb"),
        P(("groups", "gy"), "gx"),
        P("groups", "gy", "gx"),
        P(),
        P(("groups", "orb")),
    )
    out_specs = (P("groups", "gy", "gx", "orb"), P(("groups", "orb"), "gy", "gx"))
    return jax.shard_map(body, mesh=mesh, in_specs=in_specs, out_specs=out_specs, check_vma=False)
```

```python
import functools

import jax
import jax.numpy as jnp
from jax import lax
from jax.experimental import pallas as pl
from jax.experimental.pallas import tpu as pltpu
from jax.sharding import PartitionSpec as P

half_step = 0.05
DEPTH = 4
ROW_SEM = 25
MESH = pl.DeviceIdType.MESH
SIDES = ((-1, 0), (1, 0), (0, -1), (0, 1))
X0, Y0, X1, Y1, L2, LY1, L1, LY0 = range(8)


def kernel(
    sizes, x_hbm, c_hbm, onsite_ref, class_ref, table_ref, occ_ref,
    out_ref, grad_ref,
    own, fields, cf, tab, hot_ref, acc, part, part_in,
    send_rows, recv_rows, meta, meta_in, meta_mid, meta_side, meta_pad,
    copy_sem, send_sem, recv_sem,
):
    gy_n, gx_n, orb_n, rows, cols, width = sizes
    halves = width // 128
    gy, gx, orb = lax.axis_index("gy"), lax.axis_index("gx"), lax.axis_index("orb")
    d = DEPTH
    end = d + cols
    wide_cols = cols + 2 * d

    def at(si, sj):
        return {
            "gy": lax.rem(gy + si + gy_n, gy_n),
            "gx": lax.rem(gx + sj + gx_n, gx_n),
        }

    other_orb = lax.rem(orb + 1, orb_n)
    other = {"orb": other_orb}

    load_c = pltpu.make_async_copy(c_hbm, own, copy_sem.at[0])
    load_x = pltpu.make_async_copy(x_hbm, fields.at[X0, :, d:end, 0:8, :], copy_sem.at[1])
    load_c.start()
    load_x.start()

    barrier = pltpu.get_barrier_semaphore()
    for si, sj in SIDES:
        pl.semaphore_signal(barrier, inc=1, device_id=at(si, sj), device_id_type=MESH)
    pl.semaphore_signal(barrier, inc=1, device_id=other, device_id_type=MESH)

    meta[0:rows, 0:cols] = class_ref[0].astype(jnp.float32)
    meta[rows : 2 * rows, 0:cols] = class_ref[1].astype(jnp.float32)
    meta[2 * rows : 3 * rows, 0:cols] = half_step * onsite_ref[...]

    upper = lax.broadcasted_iota(jnp.int32, (8, width), 0) < 4

    def pack(f, j, c0, c1):
        turned = pltpu.roll(c1, 4, 0)
        send_rows[f, 0, j] = jnp.where(upper, c0, turned)
        send_rows[f, 1, j] = jnp.where(upper, turned, c0)

    def pack_c(j, carry):
        sign = (2 * occ_ref[...] - 1).astype(jnp.float32)
        c0, c1 = own[0, j] * sign, own[1, j] * sign
        fields[L2, 0, d + j, 0:8, :] = c0
        fields[L2, 1, d + j, 0:8, :] = c1
        pack(1, j, c0, c1)
        return carry

    def pack_x(j, carry):
        pack(0, j, fields[X0, 0, d + j, 0:8, :], fields[X0, 1, d + j, 0:8, :])
        return carry

    def remote(src, dst, n, to):
        return pltpu.make_async_remote_copy(
            src_ref=src, dst_ref=dst, send_sem=send_sem.at[n], recv_sem=recv_sem.at[n],
            device_id=to, device_id_type=MESH,
        )

    def field_copies(f, name):
        edges, copies = [], []
        for k, si in ((0, 1), (1, -1)):
            for n, (first, last) in enumerate(((0, 3), (cols - 3, cols), (3, cols - 3))):
                copy = remote(
                    send_rows.at[f, k, first:last], recv_rows.at[f, k, d + first : d + last],
                    ROW_SEM + 6 * f + 3 * k + n, at(-si, 0),
                )
                (edges if n < 2 else copies).append(copy)
        mine = fields.at[name]
        copies.append(remote(
            mine.at[:, cols:end, 0:8, :], mine.at[:, 0:d, 0:8, :], 8 * f + 6, at(0, 1)
        ))
        copies.append(remote(
            mine.at[:, d : 2 * d, 0:8, :], mine.at[:, end : end + d, 0:8, :], 8 * f + 7, at(0, -1)
        ))
        return edges, copies

    def corner_copies(f, k):
        got = recv_rows.at[f, k]
        return [
            remote(got.at[cols + 1 : end], got.at[1:d], 8 * f + 2 + k, at(0, 1)),
            remote(got.at[d : d + 3], got.at[end : end + 3], 8 * f + 4 + k, at(0, -1)),
        ]

    meta_copies = [
        remote(meta, meta_in.at[k], 16 + k, at(*to)) for k, to in enumerate(SIDES[:2])
    ]
    meta_wide = [
        remote(meta_mid, meta_side.at[k], 18 + k, at(*to)) for k, to in enumerate(SIDES[2:])
    ]
    (edges_x, copies_x), (edges_c, copies_c) = field_copies(0, X0), field_copies(1, L2)

    load_c.wait()
    lax.fori_loop(0, cols, pack_c, 0)
    pl.semaphore_wait(barrier, len(SIDES) + 1)
    for copy in meta_copies + edges_c:
        copy.start()
    load_x.wait()
    lax.fori_loop(0, cols, pack_x, 0)
    for copy in edges_x + copies_c + copies_x:
        copy.start()

    diagonal = lax.broadcasted_iota(jnp.int32, (16, 16), 0) == lax.broadcasted_iota(
        jnp.int32, (16, 16), 1
    )
    blank = jnp.zeros((16, 128), jnp.bfloat16)
    for e in range(4):
        column = jnp.sum(jnp.where(diagonal, table_ref[e : e + 1, :], 0.0), axis=1, keepdims=True)
        t = jnp.broadcast_to(half_step * column, (16, 128))
        high = t.astype(jnp.bfloat16)
        rest = t - high.astype(jnp.float32)
        mid = rest.astype(jnp.bfloat16)
        lanes = slice(e * 128, e * 128 + 128)
        tab[0:16, lanes] = high
        tab[16:32, lanes] = mid
        tab[32:48, lanes] = (rest - mid.astype(jnp.float32)).astype(jnp.bfloat16)
        tab[48:64, lanes] = blank
    for n in range(3):
        tab[16 * n : 16 * n + 16, 512:640] = blank
    tab[48:64, 512:640] = jnp.ones((16, 128), jnp.bfloat16)

    for copy in meta_copies:
        copy.wait()
    upper_tile = lax.broadcasted_iota(jnp.int32, (8, 128), 0) < 4
    for p in range(3):
        of = slice(p * rows, (p + 1) * rows)
        meta_mid[p, 0:8, :] = meta[of]
        meta_mid[p, 8:16, :] = jnp.where(upper_tile, meta_in[0, of], meta_in[1, of])
    for copy in meta_wide:
        copy.start()
    for copy in meta_wide:
        copy.wait()
    lane = lax.broadcasted_iota(jnp.int32, (16, 128), 1)
    for p in range(3):
        west = pltpu.roll(meta_side[1, p], 128 - (cols - d), 1)
        east = pltpu.roll(meta_side[0, p], end, 1)
        middle = pltpu.roll(meta_mid[p], d, 1)
        meta_pad[p] = jnp.where(lane < d, west, jnp.where(lane < end, middle, east))

    which = lax.broadcasted_iota(jnp.int32, (16, 64), 1)
    class_of = (which % 16).astype(jnp.float32)
    for j in range(wide_cols):
        lines = slice(16 * j, 16 * j + 16)
        mu = meta_pad[2, :, j : j + 1]
        high = mu.astype(jnp.bfloat16).astype(jnp.float32)
        mid = (mu - high).astype(jnp.bfloat16).astype(jnp.float32)
        low = mu - high - mid
        hot = jnp.where(meta_pad[0, :, j : j + 1] == class_of, 1.0, 0.0)
        parts = jnp.where(
            which == 48, high, jnp.where(which == 49, mid, jnp.where(which == 50, low, 0.0))
        )
        hot_ref[0, lines, :] = jnp.where(which < 48, hot, parts).astype(jnp.bfloat16)
        hot = jnp.where((meta_pad[1, :, j : j + 1] == class_of) & (which < 48), 1.0, 0.0)
        hot_ref[1, lines, :] = hot.astype(jnp.bfloat16)

    def coefficients(q, carry):
        lines = pl.ds(pl.multiple_of(64 * q, 64), 64)
        got = jnp.dot(hot_ref[0, lines, :], tab[...], preferred_element_type=jnp.float32)
        for e in range(4):
            cf[1 + e, pl.ds(4 * q, 4)] = got[:, e * 128 : e * 128 + 128].reshape(4, 16, 128)
        cf[0, pl.ds(4 * q, 4)] = got[:, 512:640].reshape(4, 16, 128)
        got = jnp.dot(hot_ref[1, lines, :], tab[:, 0:512], preferred_element_type=jnp.float32)
        for e in range(4):
            cf[5 + e, pl.ds(4 * q, 4)] = got[:, e * 128 : e * 128 + 128].reshape(4, 16, 128)
        return carry

    lax.fori_loop(0, wide_cols // 4, coefficients, 0)

    def place_halo(f, name, first, last):
        def body(j, carry):
            below, above = recv_rows[f, 0, j], recv_rows[f, 1, j]
            fields[name, 0, j, 8:16, :] = jnp.where(upper, below, above)
            fields[name, 1, j, 8:16, :] = pltpu.roll(jnp.where(upper, above, below), 4, 0)
            return carry

        lax.fori_loop(first, last, body, 0)

    def apply(src, first, last, emit):
        def body(j, carry):
            for h in range(halves):
                lanes = slice(h * 128, h * 128 + 128)
                c0, c1 = fields[src, 0, j, :, lanes], fields[src, 1, j, :, lanes]
                r0, r1 = fields[src, 0, j + 1, :, lanes], fields[src, 1, j + 1, :, lanes]
                l0, l1 = fields[src, 0, j - 1, :, lanes], fields[src, 1, j - 1, :, lanes]
                d0, d1 = pltpu.roll(c0, 15, 0), pltpu.roll(c1, 15, 0)
                mu = cf[0, j]
                b = [cf[1 + e, j] for e in range(4)]
                p = [cf[1 + e, j - 1] for e in range(4)]
                v = [cf[5 + e, j] for e in range(4)]
                w0 = mu * c1 + b[0] * r0 + b[1] * r1 + v[0] * d0 + v[1] * d1
                w0 = w0 - (p[0] * l0 + p[2] * l1) - pltpu.roll(v[0] * c0 + v[2] * c1, 1, 0)
                w1 = b[2] * r0 + b[3] * r1 + v[2] * d0 + v[3] * d1 - mu * c0
                w1 = w1 - (p[1] * l0 + p[3] * l1) - pltpu.roll(v[1] * c0 + v[3] * c1, 1, 0)
                emit(j, lanes, (w0, w1))
            return carry

        lax.fori_loop(first, last, body, 0, unroll=2)

    def plus(dst, base, factor):
        def emit(j, lanes, w):
            for c in range(2):
                moved = w[c] + w[c] if factor == 2 else w[c]
                fields[dst, c, j, :, lanes] = fields[base, c, j, :, lanes] + moved
        return emit

    def minus_twice(dst):
        def emit(j, lanes, w):
            for c in range(2):
                fields[dst, c, j, :, lanes] = -2.0 * w[c]
        return emit

    def closing(dst, base, mid):
        def emit(j, lanes, w):
            for c in range(2):
                fields[dst, c, j, :, lanes] = (
                    fields[base, c, j, :, lanes] + fields[mid, c, j, :, lanes] - w[c]
                )
        return emit

    def start_of(j, lanes, w):
        for c in range(2):
            out_ref[c, j - d, :, lanes] = (
                fields[L1, c, j, 0:8, lanes] + fields[LY0, c, j, 0:8, lanes] - w[c][0:8]
            )

    def forward(f, edges):
        corners = []
        for k in range(2):
            for copy in edges[2 * k : 2 * k + 2]:
                copy.wait_recv()
            sent = corner_copies(f, k)
            for copy in sent:
                copy.start()
            corners += sent
        return corners

    corners_c = forward(1, edges_c)
    corners_x = forward(0, edges_x)

    def arrive(f, name, copies, corners):
        for copy in corners + copies:
            copy.wait_recv()
        place_halo(f, name, 1, wide_cols - 1)

    arrive(1, L2, copies_c, corners_c)
    apply(L2, d - 3, end + 3, minus_twice(LY1))
    apply(LY1, d - 2, end + 2, closing(L1, L2, LY1))
    apply(L1, d - 1, end + 1, minus_twice(LY0))
    apply(LY0, d, end, start_of)

    arrive(0, X0, copies_x, corners_x)
    apply(X0, d - 2, end + 3, plus(Y0, X0, 1))
    apply(Y0, d - 1, end + 2, plus(X1, X0, 2))
    apply(X1, d, end + 1, plus(Y1, X1, 1))
    for copy in edges_c + copies_c + corners_c + edges_x + copies_x + corners_x:
        copy.wait_send()

    def gradient(i, carry):
        j = d + i
        sums = [jnp.zeros((8, 128), jnp.float32) for _ in range(8)]
        for h in range(halves):
            lanes = slice(h * 128, h * 128 + 128)
            for lam, val, twice in (
                (L2, Y1, True), (LY1, X1, False), (L1, Y0, True), (LY0, X0, False)
            ):
                l = [fields[lam, c, j, 0:8, lanes] for c in range(2)]
                v = [fields[val, c, j, 0:8, lanes] for c in range(2)]
                ld = [fields[lam, c, j, 1:9, lanes] for c in range(2)]
                vd = [fields[val, c, j, 1:9, lanes] for c in range(2)]
                lr = [fields[lam, c, j + 1, 0:8, lanes] for c in range(2)]
                vr = [fields[val, c, j + 1, 0:8, lanes] for c in range(2)]
                if twice:
                    v, vd, vr = ([x + x for x in group] for group in (v, vd, vr))
                for a in range(2):
                    for b in range(2):
                        e = 2 * a + b
                        sums[e] = sums[e] + (l[a] * vr[b] - v[a] * lr[b])
                        sums[4 + e] = sums[4 + e] + (l[a] * vd[b] - v[a] * ld[b])
        for e in range(8):
            acc[e, i] = sums[e]
        return carry

    lax.fori_loop(0, cols, gradient, 0, unroll=2)

    place = lax.broadcasted_iota(jnp.int32, (8, 128), 1)
    for e in range(8):
        total = jnp.zeros((8, 128), jnp.float32)
        for j in range(cols):
            total = jnp.where(place == j, jnp.sum(acc[e, j], axis=1, keepdims=True), total)
        part[e] = half_step * total
    swap = remote(part.at[pl.ds(4 * other_orb, 4)], part_in, 24, other)
    swap.start()
    swap.wait()
    total = part[pl.ds(4 * orb, 4)] + part_in[...]
    grad_ref[...] = total[:, :, 0:cols]


def on_device(sizes, checkpoint, cotangent, onsite, bond_class, bond_table, occupied):
    _, _, _, rows, cols, width = sizes
    d = DEPTH
    f32 = jnp.float32
    vmem = pl.BlockSpec(memory_space=pltpu.VMEM)
    hbm = pl.BlockSpec(memory_space=pltpu.HBM)
    start, grads = pl.pallas_call(
        functools.partial(kernel, sizes),
        out_shape=(
            jax.ShapeDtypeStruct((2, cols, rows, width), f32),
            jax.ShapeDtypeStruct((4, rows, cols), f32),
        ),
        in_specs=[hbm, hbm, vmem, vmem, vmem, vmem],
        out_specs=(vmem, vmem),
        scratch_shapes=[
            pltpu.VMEM((2, cols, rows, width), f32),
            pltpu.VMEM((8, 2, cols + 2 * d, 16, width), f32),
            pltpu.VMEM((9, cols + 2 * d, 16, 128), f32),
            pltpu.VMEM((64, 640), jnp.bfloat16),
            pltpu.VMEM((2, 16 * (cols + 2 * d), 64), jnp.bfloat16),
            pltpu.VMEM((8, cols, 8, 128), f32),
            pltpu.VMEM((8, 8, 128), f32),
            pltpu.VMEM((4, 8, 128), f32),
            pltpu.VMEM((2, 2, cols, 8, width), f32),
            pltpu.VMEM((2, 2, cols + 2 * d, 8, width), f32),
            pltpu.VMEM((3 * rows, 128), f32),
            pltpu.VMEM((2, 3 * rows, 128), f32),
            pltpu.VMEM((3, 16, 128), f32),
            pltpu.VMEM((2, 3, 16, 128), f32),
            pltpu.VMEM((3, 16, 128), f32),
            pltpu.SemaphoreType.DMA((2,)),
            pltpu.SemaphoreType.DMA((ROW_SEM + 12,)),
            pltpu.SemaphoreType.DMA((ROW_SEM + 12,)),
        ],
        compiler_params=pltpu.CompilerParams(
            collective_id=0, has_side_effects=True, vmem_limit_bytes=40 * 1024 * 1024
        ),
        cost_estimate=pl.CostEstimate(flops=60_000_000, bytes_accessed=1_500_000, transcendentals=0),
    )(
        checkpoint.transpose(0, 2, 1, 3), cotangent.transpose(0, 2, 1, 3), onsite, bond_class,
        bond_table.T, occupied.reshape(1, width),
    )
    return start.transpose(0, 2, 1, 3), grads


def solution(mesh):
    shape = mesh.shape

    def body(checkpoint, cotangent, onsite, bond_class, bond_table, occupied):
        _, rows, cols, width = checkpoint.shape
        sizes = (shape["gy"], shape["gx"], shape["orb"], rows, cols, width)
        return on_device(sizes, checkpoint, cotangent, onsite, bond_class, bond_table, occupied)

    in_specs = (
        P("groups", "gy", "gx", "orb"),
        P("groups", "gy", "gx", "orb"),
        P(("groups", "gy"), "gx"),
        P("groups", "gy", "gx"),
        P(),
        P(("groups", "orb")),
    )
    out_specs = (P("groups", "gy", "gx", "orb"), P(("groups", "orb"), "gy", "gx"))
    return jax.shard_map(body, mesh=mesh, in_specs=in_specs, out_specs=out_specs, check_vma=False)
```
